32 devices in a mesh: replica: 4 (over z), fsdp: 4 (over y, core), tensor: 2 (over x).
Axes of the slice: x: 2, y: 2, z: 4, core: 2. Of those that a mesh axis runs over, the one named last changes fastest.
Arguments:
- tokens: bfloat16 [2, 1536, 5120], P(None, ('replica', 'fsdp')), may hold values from -6 to 6
- cotangent: bfloat16 [2, 1536, 7168], P(None, 'replica', ('fsdp', 'tensor')), may hold values from -6 to 6
- gate_weight: bfloat16 [4, 5120, 7168], P('replica', None, ('fsdp', 'tensor')), may hold values from -6 to 6
- up_weight: bfloat16 [4, 5120, 7168], P('replica', None, ('fsdp', 'tensor')), may hold values from -6 to 6
Outputs:
- gate_final: bfloat16 [4, 5120, 7168], P('replica', None, ('fsdp', 'tensor'))
- up_final: bfloat16 [4, 5120, 7168], P('replica', None, ('fsdp', 'tensor'))
The draws below stay inside these ranges and needn't reach their ends.
All inputs are finite; a program needn't handle non-finite values.
Results may differ from the reference program's by a relative error of at most 0.0052.
Values may be sent and summed in bfloat16 or wider, within the bound.
A program may use at most 256 MiB of HBM per device.

```python
import jax
import jax.numpy as jnp
from jax import lax

D = 5120
FF = 7168
STEPS = 2
REPLICAS = 4
TOK_REP = 384
TOKENS = 1536


def shard_levels(key, shape, shards, low, high):
    def one(axis_at, shards_of):
        steps = jax.random.uniform(jax.random.fold_in(jax.random.fold_in(key, 6), axis_at), (shards_of,), jnp.float32, low / len(shards), high / len(shards))
        return jnp.repeat(jnp.exp(steps), shape[axis_at] // shards_of).reshape((-1,) + (1,) * (len(shape) - axis_at - 1))

    loudness = one(*shards[0])
    for cut in shards[1:]:
        loudness = loudness * one(*cut)
    return loudness


def gaussian(own_key, dims, spread, reach, split=(), kind=jnp.bfloat16):
    result = spread * jax.random.normal(own_key, dims, jnp.float32)
    if split:
        result = result * shard_levels(own_key, dims, split, -0.22, 0.18)
    return jnp.clip(result, -reach, reach).astype(kind)


def setup_inputs(seed: int = 0) -> dict:
    seeds = jax.random.split(jax.random.key(seed), 5)
    tokens = gaussian(seeds[0], (STEPS, TOKENS, D), 1.0, 6.0, ((1, 16),))
    cotangent = gaussian(seeds[1], (STEPS, TOKENS, FF), 1.0, 6.0, ((1, 4), (2, 8)))
    gate_weight = gaussian(seeds[2], (REPLICAS, D, FF), 1.0, 6.0, ((0, 4), (2, 8)))
    up_weight = gaussian(seeds[3], (REPLICAS, D, FF), 1.0, 6.0, ((0, 4), (2, 8)))
    return {"tokens": tokens, "cotangent": cotangent, "gate_weight": gate_weight, "up_weight": up_weight}


learn_rate = 1.0


def replica_update(inputs, upstream, gate_w, up_w):
    factor = float(D) ** -0.5
    gate_pre = jnp.dot(inputs, gate_w, preferred_element_type=jnp.float32) * factor
    up_pre = jnp.dot(inputs, up_w, preferred_element_type=jnp.float32) * factor
    logistic = jax.nn.sigmoid(gate_pre)
    grad_in = upstream.astype(jnp.float32)
    d_up = (grad_in * gate_pre * logistic).astype(jnp.bfloat16)
    d_gate = (grad_in * up_pre * logistic * (1.0 + gate_pre * (1.0 - logistic))).astype(jnp.bfloat16)
    grad_gate = jnp.dot(inputs.T, d_gate, preferred_element_type=jnp.float32) * factor
    grad_up = jnp.dot(inputs.T, d_up, preferred_element_type=jnp.float32) * factor
    return gate_w.astype(jnp.float32) - learn_rate * grad_gate, up_w.astype(jnp.float32) - learn_rate * grad_up


def reference(tokens, cotangent, gate_weight, up_weight):
    gate_now, up_now = gate_weight, up_weight
    for section in range(STEPS):
        inputs = tokens[section].reshape(REPLICAS, TOK_REP, D)
        upstream = cotangent[section].reshape(REPLICAS, TOK_REP, FF)
        own_gate, own_up = lax.map(lambda item: replica_update(*item), (inputs, upstream, gate_now, up_now))
        partners = jnp.arange(REPLICAS, dtype=jnp.int32) ^ (1 << section)
        gate_next = (0.5 * own_gate + 0.5 * gate_now[partners].astype(jnp.float32)).astype(jnp.bfloat16)
        up_next = (0.5 * own_up + 0.5 * up_now[partners].astype(jnp.float32)).astype(jnp.bfloat16)
        gate_now, up_now = gate_next, up_next
    return gate_now, up_now
```

```python
import jax
import jax.numpy as jnp
from jax import lax
from jax.sharding import PartitionSpec as P

learn_rate = 1.0
GROUP = 4
CHUNKS = 20


def swap(value, mask):
    pairs = [(source, source ^ mask) for source in range(lax.axis_size("replica"))]
    return lax.ppermute(value, "replica", pairs)


def shift(value, by):
    pairs = [
        (source, source + by)
        for source in range(lax.axis_size("replica"))
        if 0 <= source % GROUP + by < GROUP
    ]
    return lax.ppermute(value, "replica", pairs)


def f32_dot(a, b):
    return jnp.dot(a, b, preferred_element_type=jnp.float32)


def backward(gate_pre, up_pre, upstream):
    logistic = jax.nn.sigmoid(gate_pre)
    grad_in = upstream.astype(jnp.float32)
    d_up = (grad_in * gate_pre * logistic).astype(jnp.bfloat16)
    d_gate = (grad_in * up_pre * logistic * (1.0 + gate_pre * (1.0 - logistic))).astype(
        jnp.bfloat16
    )
    return d_gate, d_up


def per_device(tokens, cotangent, gate_weight, up_weight):
    weights = (gate_weight[0], up_weight[0])
    depth, width = weights[0].shape
    factor = float(depth) ** (-0.5)
    place = lax.axis_index("replica") % GROUP
    rows = depth // CHUNKS

    moved = jnp.stack([swap(tokens[0], 2), swap(tokens[1], 1)])
    own = lax.all_gather(tokens, "fsdp", axis=1, tiled=True)
    moved = lax.all_gather(moved, "fsdp", axis=1, tiled=True)
    x0, x1 = own[0], own[1]
    x0_far, x1_near = moved[0], moved[1]

    near = [swap(f32_dot(x1_near, w).astype(jnp.bfloat16), 1) for w in weights]
    d0 = backward(*[f32_dot(x0, w) * factor for w in weights], cotangent[0])
    d0_far = [swap(d, 2) for d in d0]
    cross = f32_dot(x1, x0.T)
    cross_hi = cross.astype(jnp.bfloat16)
    cross_lo = (cross - cross_hi.astype(jnp.float32)).astype(jnp.bfloat16)
    pre1 = []
    for w, n, d in zip(weights, near, d0):
        drift = (f32_dot(cross_hi, d) + f32_dot(cross_lo, d)) * (learn_rate * factor)
        pre1.append((0.5 * factor) * (f32_dot(x1, w) + n.astype(jnp.float32) - drift))
    d1 = backward(*pre1, cotangent[1])
    lefts = jnp.concatenate([x0, x0_far, x1], axis=0)
    rights = [
        jnp.concatenate([a, b, 2.0 * c], axis=0) for a, b, c in zip(d0, d0_far, d1)
    ]

    def piece(w, index):
        index = jnp.clip(index, 0, CHUNKS - 1)
        return lax.dynamic_slice_in_dim(w, index * rows, rows, axis=0)

    arrived = {(m, by): [] for m in range(2) for by in (1, -1)}
    for step in range(CHUNKS + GROUP - 2):
        for m in range(2):
            for by in (1, -1):
                rank = place if by == 1 else GROUP - 1 - place
                block = piece(weights[m], step - rank)
                if step:
                    before = arrived[m, by][-1].astype(jnp.float32)
                    block = (before + block.astype(jnp.float32)).astype(jnp.bfloat16)
                arrived[m, by].append(shift(block, by))

    outs = []
    for m in range(2):
        parts = []
        for chunk in range(CHUNKS):
            total = weights[m][chunk * rows : (chunk + 1) * rows].astype(jnp.float32)
            for by in (1, -1):
                rank = place if by == 1 else GROUP - 1 - place
                zero = jnp.zeros((rows, width), jnp.bfloat16)
                total = total + lax.select_n(
                    rank, zero, *[arrived[m, by][chunk + i] for i in range(GROUP - 1)]
                ).astype(jnp.float32)
            x = lefts[:, chunk * rows : (chunk + 1) * rows]
            grad = f32_dot(x.T, rights[m])
            parts.append((0.25 * total - (0.25 * learn_rate * factor) * grad).astype(jnp.bfloat16))
        outs.append(jnp.concatenate(parts, axis=0)[None])
    return tuple(outs)


def solution(mesh):
    return jax.shard_map(
        per_device,
        mesh=mesh,
        in_specs=(
            P(None, ("replica", "fsdp"), None),
            P(None, "replica", ("fsdp", "tensor")),
            P("replica", None, ("fsdp", "tensor")),
            P("replica", None, ("fsdp", "tensor")),
        ),
        out_specs=(P("replica", None, ("fsdp", "tensor")), P("replica", None, ("fsdp", "tensor"))),
        check_vma=False,
    )
```

```python
import jax
import jax.numpy as jnp
from jax import lax
from jax.sharding import PartitionSpec as P

learn_rate = 1.0
GROUP = 4
CHUNKS = 20
FIRST_STEP = 4


def swap(value, mask):
    pairs = [(source, source ^ mask) for source in range(lax.axis_size("replica"))]
    return lax.ppermute(value, "replica", pairs)


def shift(value, by, step):
    pairs = []
    for source in range(lax.axis_size("replica")):
        place = source % GROUP
        rank = place if by == 1 else GROUP - 1 - place
        if 0 <= place + by < GROUP and 0 <= step - rank < CHUNKS:
            pairs.append((source, source + by))
    return lax.ppermute(value, "replica", pairs)


def gather_moved(value, mask):
    share = value.shape[0] // lax.axis_size("tensor")
    part = lax.dynamic_slice_in_dim(value, lax.axis_index("tensor") * share, share, axis=0)
    return lax.all_gather(swap(part, mask), ("fsdp", "tensor"), axis=0, tiled=True)


def f32_dot(a, b):
    return jnp.dot(a, b, preferred_element_type=jnp.float32)


def backward(gate_pre, up_pre, upstream):
    logistic = jax.nn.sigmoid(gate_pre)
    grad_in = upstream.astype(jnp.float32)
    d_up = (grad_in * gate_pre * logistic).astype(jnp.bfloat16)
    d_gate = (grad_in * up_pre * logistic * (1.0 + gate_pre * (1.0 - logistic))).astype(
        jnp.bfloat16
    )
    return d_gate, d_up


def per_device(tokens, cotangent, gate_weight, up_weight):
    weights = (gate_weight[0], up_weight[0])
    depth, width = weights[0].shape
    factor = float(depth) ** (-0.5)
    place = lax.axis_index("replica") % GROUP
    rows = depth // CHUNKS

    x1_near = gather_moved(tokens[1], 1)
    x0 = lax.all_gather(tokens[0], "fsdp", axis=0, tiled=True)
    x0_far = gather_moved(tokens[0], 2)
    x1 = lax.all_gather(tokens[1], "fsdp", axis=0, tiled=True)

    def piece(w, index):
        index = jnp.clip(index, 0, CHUNKS - 1)
        return lax.dynamic_slice_in_dim(w, index * rows, rows, axis=0)

    arrived = {(m, by): [] for m in range(2) for by in (1, -1)}
    ranks = {1: place, -1: GROUP - 1 - place}
    zero = jnp.zeros((rows, width), jnp.bfloat16)

    def final(out, m, chunk):
        start = chunk * rows
        total = weights[m][start : start + rows].astype(jnp.float32)
        for by in (1, -1):
            total = total + lax.select_n(
                ranks[by], zero, *[arrived[m, by][chunk + i] for i in range(GROUP - 1)]
            ).astype(jnp.float32)
        grad = f32_dot(lefts[:, start : start + rows].T, rights[m])
        value = 0.25 * total - (0.25 * learn_rate * factor) * grad
        return lax.dynamic_update_slice_in_dim(out, value.astype(jnp.bfloat16), start, axis=0)

    outs = [jnp.zeros((depth, width), jnp.bfloat16) for _ in range(2)]
    done = 0
    near, products = [], []
    for step in range(CHUNKS + GROUP - 2):
        ready = done
        if step > FIRST_STEP + 4:
            ready = max(done, min(done + 2, step - GROUP + 1, CHUNKS))
        for m in range(2):
            blocks = []
            for by in (1, -1):
                block = piece(weights[m], step - ranks[by])
                if step:
                    before = arrived[m, by][-1].astype(jnp.float32)
                    block = (before + block.astype(jnp.float32)).astype(jnp.bfloat16)
                blocks.append(block)
            at = (step - FIRST_STEP, m)
            if at == (0, 0):
                gate_pre0 = f32_dot(x0, weights[0]) * factor
                blocks, gate_pre0 = lax.optimization_barrier((blocks, gate_pre0))
            if at == (0, 1):
                d0 = backward(gate_pre0, f32_dot(x0, weights[1]) * factor, cotangent[0])
                blocks, d0 = lax.optimization_barrier((blocks, d0))
                d0_far = [swap(d, 2) for d in d0]
            if at[0] == 1:
                part = f32_dot(x1_near, weights[m]).astype(jnp.bfloat16)
                blocks, part = lax.optimization_barrier((blocks, part))
                near.append(swap(part, 1))
            if at == (2, 0):
                cross = f32_dot(x1, x0.T)
                cross_hi = cross.astype(jnp.bfloat16)
                cross_lo = (cross - cross_hi.astype(jnp.float32)).astype(jnp.bfloat16)
                blocks, cross_hi, cross_lo = lax.optimization_barrier(
                    (blocks, cross_hi, cross_lo)
                )
            if at[0] == 3:
                product = f32_dot(x1, weights[m])
                blocks, product = lax.optimization_barrier((blocks, product))
                products.append(product)
            if at == (4, 0):
                pre1 = []
                for product, n, d in zip(products, near, d0):
                    drift = f32_dot(cross_hi, d) + f32_dot(cross_lo, d)
                    pre1.append(
                        (0.5 * factor)
                        * (product + n.astype(jnp.float32) - (learn_rate * factor) * drift)
                    )
                d1 = backward(*pre1, cotangent[1])
                blocks, d1 = lax.optimization_barrier((blocks, d1))
            if at == (4, 1):
                lefts = jnp.concatenate([x0, x0_far, x1], axis=0)
                rights = [
                    jnp.concatenate([a, b, 2.0 * c], axis=0)
                    for a, b, c in zip(d0, d0_far, d1)
                ]
                blocks, lefts, rights = lax.optimization_barrier((blocks, lefts, rights))
            if ready > done:
                for chunk in range(done, ready):
                    outs[m] = final(outs[m], m, chunk)
                blocks, outs[m] = lax.optimization_barrier((blocks, outs[m]))
            for by, block in zip((1, -1), blocks):
                arrived[m, by].append(shift(block, by, step))
        done = ready
    for m in range(2):
        for chunk in range(done, CHUNKS):
            outs[m] = final(outs[m], m, chunk)
    return tuple(out[None] for out in outs)


def solution(mesh):
    return jax.shard_map(
        per_device,
        mesh=mesh,
        in_specs=(
            P(None, ("replica", "fsdp"), None),
            P(None, "replica", ("fsdp", "tensor")),
            P("replica", None, ("fsdp", "tensor")),
            P("replica", None, ("fsdp", "tensor")),
        ),
        out_specs=(P("replica", None, ("fsdp", "tensor")), P("replica", None, ("fsdp", "tensor"))),
        check_vma=False,
    )
```

```python
import jax
import jax.numpy as jnp
from jax import lax
from jax.sharding import PartitionSpec as P

learn_rate = 1.0
GROUP = 4
CHUNKS = 10
FIRST_STEP = 2


def swap(value, mask):
    pairs = [(source, source ^ mask) for source in range(lax.axis_size("replica"))]
    return lax.ppermute(value, "replica", pairs)


def shift(value, by, step):
    pairs = []
    for source in range(lax.axis_size("replica")):
        place = source % GROUP
        rank = place if by == 1 else GROUP - 1 - place
        if 0 <= place + by < GROUP and 0 <= step - rank < CHUNKS:
            pairs.append((source, source + by))
    return lax.ppermute(value, "replica", pairs)


def gather_moved(value, mask):
    share = value.shape[0] // lax.axis_size("tensor")
    part = lax.dynamic_slice_in_dim(value, lax.axis_index("tensor") * share, share, axis=0)
    return lax.all_gather(swap(part, mask), ("fsdp", "tensor"), axis=0, tiled=True)


def f32_dot(a, b):
    return jnp.dot(a, b, preferred_element_type=jnp.float32)


def backward(gate_pre, up_pre, upstream):
    logistic = jax.nn.sigmoid(gate_pre)
    grad_in = upstream.astype(jnp.float32)
    d_up = (grad_in * gate_pre * logistic).astype(jnp.bfloat16)
    d_gate = (grad_in * up_pre * logistic * (1.0 + gate_pre * (1.0 - logistic))).astype(
        jnp.bfloat16
    )
    return d_gate, d_up


def per_device(tokens, cotangent, gate_weight, up_weight):
    weights = (gate_weight[0], up_weight[0])
    depth, width = weights[0].shape
    factor = float(depth) ** (-0.5)
    place = lax.axis_index("replica") % GROUP
    rows = depth // CHUNKS

    x1_near = gather_moved(tokens[1], 1)
    x0 = lax.all_gather(tokens[0], "fsdp", axis=0, tiled=True)
    x0_far = gather_moved(tokens[0], 2)
    x1 = lax.all_gather(tokens[1], "fsdp", axis=0, tiled=True)

    def piece(w, index):
        index = jnp.clip(index, 0, CHUNKS - 1)
        return lax.dynamic_slice_in_dim(w, index * rows, rows, axis=0)

    arrived = {(m, by): [] for m in range(2) for by in (1, -1)}
    ranks = {1: place, -1: GROUP - 1 - place}
    zero = jnp.zeros((rows, width), jnp.bfloat16)

    def final(out, m, chunk):
        start = chunk * rows
        total = weights[m][start : start + rows].astype(jnp.float32)
        for by in (1, -1):
            total = total + lax.select_n(
                ranks[by], zero, *[arrived[m, by][chunk + i] for i in range(GROUP - 1)]
            ).astype(jnp.float32)
        grad = f32_dot(lefts[:, start : start + rows].T, rights[m])
        value = 0.25 * total - (0.25 * learn_rate * factor) * grad
        return lax.dynamic_update_slice_in_dim(out, value.astype(jnp.bfloat16), start, axis=0)

    outs = [jnp.zeros((depth, width), jnp.bfloat16) for _ in range(2)]
    done = 0
    near, products = [], []
    for step in range(CHUNKS + GROUP - 2):
        ready = done
        if step > FIRST_STEP + 4:
            ready = max(done, min(done + 2, step - GROUP + 1, CHUNKS))
        for m in range(2):
            blocks = []
            for by in (1, -1):
                block = piece(weights[m], step - ranks[by])
                if step:
                    before = arrived[m, by][-1].astype(jnp.float32)
                    block = (before + block.astype(jnp.float32)).astype(jnp.bfloat16)
                blocks.append(block)
            at = (step - FIRST_STEP, m)
            if at == (0, 0):
                gate_pre0 = f32_dot(x0, weights[0]) * factor
                blocks, gate_pre0 = lax.optimization_barrier((blocks, gate_pre0))
            if at == (0, 1):
                d0 = backward(gate_pre0, f32_dot(x0, weights[1]) * factor, cotangent[0])
                blocks, d0 = lax.optimization_barrier((blocks, d0))
                d0_far = [swap(d, 2) for d in d0]
            if at[0] == 1:
                part = f32_dot(x1_near, weights[m]).astype(jnp.bfloat16)
                blocks, part = lax.optimization_barrier((blocks, part))
                near.append(swap(part, 1))
            if at == (2, 0):
                cross = f32_dot(x1, x0.T)
                cross_hi = cross.astype(jnp.bfloat16)
                cross_lo = (cross - cross_hi.astype(jnp.float32)).astype(jnp.bfloat16)
                blocks, cross_hi, cross_lo = lax.optimization_barrier(
                    (blocks, cross_hi, cross_lo)
                )
            if at[0] == 3:
                product = f32_dot(x1, weights[m])
                blocks, product = lax.optimization_barrier((blocks, product))
                products.append(product)
            if at == (4, 0):
                pre1 = []
                for product, n, d in zip(products, near, d0):
                    drift = f32_dot(cross_hi, d) + f32_dot(cross_lo, d)
                    pre1.append(
                        (0.5 * factor)
                        * (product + n.astype(jnp.float32) - (learn_rate * factor) * drift)
                    )
                d1 = backward(*pre1, cotangent[1])
                blocks, d1 = lax.optimization_barrier((blocks, d1))
            if at == (4, 1):
                lefts = jnp.concatenate([x0, x0_far, x1], axis=0)
                rights = [
                    jnp.concatenate([a, b, 2.0 * c], axis=0)
                    for a, b, c in zip(d0, d0_far, d1)
                ]
                blocks, lefts, rights = lax.optimization_barrier((blocks, lefts, rights))
            if ready > done:
                for chunk in range(done, ready):
                    outs[m] = final(outs[m], m, chunk)
                blocks, outs[m] = lax.optimization_barrier((blocks, outs[m]))
            for by, block in zip((1, -1), blocks):
                arrived[m, by].append(shift(block, by, step))
        done = ready
    for m in range(2):
        for chunk in range(done, CHUNKS):
            outs[m] = final(outs[m], m, chunk)
    return tuple(out[None] for out in outs)


def solution(mesh):
    return jax.shard_map(
        per_device,
        mesh=mesh,
        in_specs=(
            P(None, ("replica", "fsdp"), None),
            P(None, "replica", ("fsdp", "tensor")),
            P("replica", None, ("fsdp", "tensor")),
            P("replica", None, ("fsdp", "tensor")),
        ),
        out_specs=(P("replica", None, ("fsdp", "tensor")), P("replica", None, ("fsdp", "tensor"))),
        check_vma=False,
    )
```
